32 devices in a mesh: hours: 2 (over x), lon: 8 (over z, y), lat: 2 (over core).
Axes of the slice: x: 2, y: 2, z: 4, core: 2. Of those that a mesh axis runs over, the one named last changes fastest.
Arguments:
- field: float32 [16, 512, 2048], P('hours', 'lon', 'lat'), parts along dimension 0, may hold values from -6 to 6
- longitude_matrix: float32 [1024, 512], P(('hours', 'lon')), parts along dimension 0, may hold values from -0.25 to 0.25
- latitude_matrix: float32 [4096, 256], P(('hours', 'lat')), parts along dimension 0, may hold values from -0.125 to 0.125
Outputs:
- core: float32 [16, 512, 256], P('hours', 'lon', 'lat'), parts along dimension 0
The draws below stay inside these ranges and needn't reach their ends.
There are 2 independent parts, one for each index of `hours`. The reference program is written for one: setup_inputs(seed, part) draws one part's arguments, and reference() takes and returns one part's arrays. A program takes and returns all parts, laid end to end along the dimension named above; each array names one. Nothing has to cross between parts.
All inputs are finite; a program needn't handle non-finite values.
Results may differ from the reference program's by a relative error of at most 0.000073.
Values sent between devices are 32-bit elements; how exact they have to be, the bound alone decides.
A program may use at most 64 MiB of HBM per device.

```python
import jax
import jax.numpy as jnp
from jax import lax

LEVELS = 8
RLON = 512
RLAT = 256
NLON = 512
NLAT = 2048


def shard_levels(stream_key, dims, cuts, least, top_value):
    factor_of, own = 1.0, jax.random.fold_in(stream_key, 6)
    for position, parts in cuts:
        steps = jnp.exp(jax.random.uniform(jax.random.fold_in(own, position), (parts,), jnp.float32, least / len(cuts), top_value / len(cuts)))
        factor_of = factor_of * jnp.repeat(steps, dims[position] // parts).reshape([-1 if axis == position else 1 for axis in range(len(dims))])
    return factor_of


def scatter_about(key, extent, deviation, bound, split=(), dtype=jnp.bfloat16):
    gain = shard_levels(key, extent, split, -0.22, 0.18) if split else 1.0
    array = jax.random.normal(key, extent, jnp.float32) * deviation * gain
    return jnp.minimum(jnp.maximum(array, -bound), bound).astype(dtype)


def setup_inputs(seed: int = 0, part: int = 0) -> dict:
    key_list = jax.random.split(jax.random.key(seed), 4)
    part_keys = jax.random.split(jax.random.fold_in(key_list[3], part), 4)
    field = scatter_about(part_keys[0], (LEVELS, NLON, NLAT), 1.0, 6.0, ((1, 8), (2, 2)), jnp.float32)
    longitude_matrix = scatter_about(part_keys[1], (NLON, RLON), NLON ** -0.5, 0.25, ((0, 8),), jnp.float32)
    latitude_matrix = scatter_about(part_keys[2], (NLAT, RLAT), NLAT ** -0.5, 0.125, ((0, 2),), jnp.float32)
    return dict(field=field, longitude_matrix=longitude_matrix, latitude_matrix=latitude_matrix)


def reference(field, longitude_matrix, latitude_matrix):
    highest_precision = lax.Precision.HIGHEST
    latitude_partial_sum = jnp.einsum('vnm,mb->vnb', field, latitude_matrix, precision=highest_precision)
    return jnp.einsum('ucs,ch->uhs', latitude_partial_sum, longitude_matrix, precision=highest_precision)
```

```python
import functools

import jax
import jax.numpy as jnp
from jax import lax
from jax.experimental import pallas as pl
from jax.experimental.pallas import tpu as pltpu
from jax.sharding import PartitionSpec as P

F32 = jnp.float32
BF16 = jnp.bfloat16


def split(x):
    hi = x.astype(BF16)
    return hi, (x - hi.astype(F32)).astype(BF16)


def dot(a, b):
    return jnp.dot(a, b, preferred_element_type=F32)


def kernel(
    chunks, y_size,
    field_hbm, lon_hbm, lat_hbm, out_ref,
    field_buf, lat_buf, lon_buf, lat_hi, lat_lo, lon_hi, lon_lo,
    mine, sent, got, level_buf, core_buf,
    field_sem, lat_sem, lon_sem, pair_send, pair_recv,
    lon_send, lon_recv, share_send, share_recv,
    one_send, one_recv, two_send, two_recv,
):
    levels, rows, depth = field_buf.shape
    width = mine.shape[2]
    peers = levels
    half = rows // 2
    z_size = peers // y_size
    per = levels // chunks
    me = lax.axis_index("lon")
    core = lax.axis_index("lat")
    other = 1 - core
    z, y = me // y_size, lax.rem(me, y_size)

    def remote(src, dst, send_sem, recv_sem, target):
        return pltpu.make_async_remote_copy(
            src_ref=src, dst_ref=dst, send_sem=send_sem, recv_sem=recv_sem,
            device_id=target, device_id_type=pl.DeviceIdType.MESH,
        )

    my_half = pl.ds(pl.multiple_of(core * half, half), half)
    lon_in = pltpu.make_async_copy(lon_hbm.at[my_half], lon_buf.at[me, my_half], lon_sem)
    lon_in.start()
    lat_in = []
    for part, who in ((0, core), (1, other)):
        columns = pl.ds(pl.multiple_of(who * width, width), width)
        copy = pltpu.make_async_copy(
            lat_hbm.at[:, columns], lat_buf.at[:, pl.ds(part * width, width)], lat_sem.at[part]
        )
        copy.start()
        lat_in.append(copy)
    field_in = []
    for c in range(chunks):
        span = pl.ds(c * per, per)
        copy = pltpu.make_async_copy(field_hbm.at[span], field_buf.at[span], field_sem.at[c])
        copy.start()
        field_in.append(copy)

    barrier = pltpu.get_barrier_semaphore()
    for d in range(1, peers):
        pl.semaphore_signal(
            barrier, inc=1, device_id={"lon": lax.rem(me + d, peers)}, device_id_type=pl.DeviceIdType.MESH
        )
    pl.semaphore_signal(barrier, inc=1, device_id={"lat": other}, device_id_type=pl.DeviceIdType.MESH)
    pl.semaphore_wait(barrier, peers)

    def lon_copy(shard, slot, target):
        ref = lon_buf.at[shard, my_half]
        return remote(ref, ref, lon_send.at[slot], lon_recv.at[shard], {"lon": target})

    mate = z * y_size + (1 - y)
    lon_in.wait()
    started = []
    for d in range(1, z_size):
        started.append(lon_copy(me, d - 1, lax.rem(z + d, z_size) * y_size + y))
    started.append(lon_copy(me, z_size - 1, mate))
    for copy in started:
        copy.start()

    for copy in lat_in:
        copy.wait()
    hi, lo = split(lat_buf[...])
    lat_hi[...] = hi
    lat_lo[...] = lo
    pair = []
    for c in range(chunks):
        field_in[c].wait()
        span = pl.ds(c * per, per)
        hi, lo = split(field_buf[span].reshape(per * rows, depth))
        total = dot(hi, lat_hi[...]) + dot(hi, lat_lo[...]) + dot(lo, lat_hi[...])
        sent[span] = total[:, width:].reshape(per, rows, width)
        copy = remote(sent.at[span], got.at[span], pair_send.at[c], pair_recv.at[c], {"lat": other})
        copy.start()
        pair.append(copy)
        mine[span] = total[:, :width].reshape(per, rows, width)

    def one_copy(level):
        return remote(mine.at[level], level_buf.at[me], one_send.at[level], one_recv.at[me], {"lon": level})

    for c in range(chunks):
        pair[c].wait_recv()
        span = pl.ds(c * per, per)
        mine[span] = mine[span] + got[span]
        for level in range(c * per, (c + 1) * per):
            @pl.when(me != level)
            def _():
                one_copy(level).start()

            @pl.when(me == level)
            def _():
                level_buf[level] = mine[level]

    def lon_arrived(shard):
        ref = lon_buf.at[shard, my_half]
        remote(ref, ref, lon_send.at[0], lon_recv.at[shard], {"lon": mate}).wait_recv()

    for d in range(1, z_size):
        shard = lax.rem(z + d, z_size) * y_size + y
        lon_arrived(shard)
        copy = lon_copy(shard, z_size - 1 + d, mate)
        copy.start()
        started.append(copy)
    for d in range(z_size):
        lon_arrived(lax.rem(z + d, z_size) * y_size + (1 - y))
    all_halves = lon_buf.at[:, my_half]
    share = remote(all_halves, all_halves, share_send, share_recv, {"lat": other})
    share.start()
    share.wait_recv()
    step = lon_hi.shape[1] // 4
    for block in range(lon_hi.shape[0] // step):
        cols = pl.ds(block * step, step)
        hi, lo = split(lon_buf[:, :, cols].reshape(peers * rows, step).T)
        lon_hi[cols] = hi
        lon_lo[cols] = lo

    for d in range(1, peers):
        source = lax.rem(me + d, peers)
        remote(mine.at[0], level_buf.at[source], one_send.at[0], one_recv.at[source], {"lon": source}).wait_recv()
    hi, lo = split(level_buf[...].reshape(peers * rows, width))
    core_buf[...] = (
        dot(lon_hi[...], hi) + dot(lon_hi[...], lo) + dot(lon_lo[...], hi)
    ).reshape(core_buf.shape)

    def two_copy(target):
        return remote(core_buf.at[target], out_ref.at[me], two_send.at[target], two_recv.at[me], {"lon": target})

    for d in range(1, peers):
        two_copy(lax.rem(me + d, peers)).start()
    out_ref[me] = core_buf[me]

    for copy in started:
        copy.wait_send()
    share.wait_send()
    for copy in pair:
        copy.wait_send()
    for d in range(1, peers):
        one_copy(lax.rem(me + d, peers)).wait_send()
    for d in range(1, peers):
        source = lax.rem(me + d, peers)
        remote(core_buf.at[0], out_ref.at[source], two_send.at[0], two_recv.at[source], {"lon": source}).wait_recv()
    for d in range(1, peers):
        two_copy(lax.rem(me + d, peers)).wait_send()


def exchanged(field, longitude_matrix, latitude_matrix):
    levels, rows, depth = field.shape
    rank = longitude_matrix.shape[1]
    columns = latitude_matrix.shape[1]
    peers = lax.axis_size("lon")
    width = columns // lax.axis_size("lat")
    block = rank // peers
    chunks, y_size = 2, 2
    z_size = peers // y_size
    dma = pltpu.SemaphoreType.DMA
    flops = 6 * (levels * rows * depth * columns + peers * rows * rank * width)
    return pl.pallas_call(
        functools.partial(kernel, chunks, y_size),
        out_shape=jax.ShapeDtypeStruct((levels, block, width), F32),
        in_specs=[pl.BlockSpec(memory_space=pltpu.HBM)] * 3,
        out_specs=pl.BlockSpec(memory_space=pltpu.VMEM),
        scratch_shapes=[
            pltpu.VMEM((levels, rows, depth), F32),
            pltpu.VMEM((depth, columns), F32),
            pltpu.VMEM((peers, rows, rank), F32),
            pltpu.VMEM((depth, columns), BF16),
            pltpu.VMEM((depth, columns), BF16),
            pltpu.VMEM((rank, peers * rows), BF16),
            pltpu.VMEM((rank, peers * rows), BF16),
            pltpu.VMEM((levels, rows, width), F32),
            pltpu.VMEM((levels, rows, width), F32),
            pltpu.VMEM((levels, rows, width), F32),
            pltpu.VMEM((peers, rows, width), F32),
            pltpu.VMEM((peers, block, width), F32),
            dma((chunks,)), dma((2,)), dma(()), dma((chunks,)), dma((chunks,)),
            dma((2 * z_size - 1,)), dma((peers,)), dma(()), dma(()),
            dma((peers,)), dma((peers,)), dma((peers,)), dma((peers,)),
        ],
        compiler_params=pltpu.CompilerParams(
            collective_id=0, has_side_effects=True, vmem_limit_bytes=40 * 1024 * 1024
        ),
        cost_estimate=pl.CostEstimate(
            flops=flops, bytes_accessed=4 * (field.size + longitude_matrix.size + latitude_matrix.size), transcendentals=0
        ),
    )(field, longitude_matrix, latitude_matrix)


def collected(field, longitude_matrix, latitude_matrix):
    highest = lax.Precision.HIGHEST
    reduced = lax.psum_scatter(
        jnp.einsum("mb,vnm->bvn", latitude_matrix, field, precision=highest),
        "lat", scatter_dimension=0, tiled=True,
    )
    parts = lax.psum_scatter(
        jnp.einsum("bvn,na->avb", reduced, longitude_matrix, precision=highest),
        "lon", scatter_dimension=0, tiled=True,
    )
    return jnp.transpose(parts, (1, 0, 2))


def body(field, longitude_matrix, latitude_matrix):
    if lax.axis_size("lat") == 2 and lax.axis_size("lon") == 8 == field.shape[0]:
        return exchanged(field, longitude_matrix, latitude_matrix)
    return collected(field, longitude_matrix, latitude_matrix)


def solution(mesh):
    in_specs = (P("hours", "lon", "lat"), P(("hours", "lon"), None), P(("hours", "lat"), None))
    out_specs = P("hours", "lon", "lat")
    return jax.shard_map(body, mesh=mesh, in_specs=in_specs, out_specs=out_specs, check_vma=False)
```

```python
import functools

import jax
import jax.numpy as jnp
from jax import lax
from jax.experimental import pallas as pl
from jax.experimental.pallas import tpu as pltpu
from jax.sharding import PartitionSpec as P

F32 = jnp.float32
BF16 = jnp.bfloat16


def split(x):
    hi = x.astype(BF16)
    return hi, (x - hi.astype(F32)).astype(BF16)


def dot(a, b):
    return jnp.dot(a, b, preferred_element_type=F32)


def kernel(
    chunks, y_size,
    field_hbm, lon_hbm, lat_hbm, out_ref,
    field_buf, lat_buf, lon_buf, lat_hi, lat_lo, lon_hi, lon_lo,
    mine, sent, got, level_buf, core_buf,
    field_sem, lat_sem, lon_sem, pair_send, pair_recv,
    lon_send, lon_recv, share_send, share_recv,
    one_send, one_recv, two_send, two_recv,
):
    levels, rows, depth = field_buf.shape
    width = mine.shape[2]
    peers = levels
    half = rows // 2
    z_size = peers // y_size
    per = levels // chunks
    me = lax.axis_index("lon")
    core = lax.axis_index("lat")
    other = 1 - core
    z, y = me // y_size, lax.rem(me, y_size)

    def flipped(along, across):
        z_there = (z, z + 1 - 2 * lax.rem(z, 2), lax.rem(z + 2, z_size), z_size - 1 - z)[along]
        return z_there, (y, 1 - y)[across]

    def remote(src, dst, send_sem, recv_sem, target):
        return pltpu.make_async_remote_copy(
            src_ref=src, dst_ref=dst, send_sem=send_sem, recv_sem=recv_sem,
            device_id=target, device_id_type=pl.DeviceIdType.MESH,
        )

    my_half = pl.ds(pl.multiple_of(core * half, half), half)
    lon_in = pltpu.make_async_copy(lon_hbm.at[my_half], lon_buf.at[me, my_half], lon_sem)
    lon_in.start()
    lat_in = []
    for part, who in ((0, core), (1, other)):
        columns = pl.ds(pl.multiple_of(who * width, width), width)
        copy = pltpu.make_async_copy(
            lat_hbm.at[:, columns], lat_buf.at[:, pl.ds(part * width, width)], lat_sem.at[part]
        )
        copy.start()
        lat_in.append(copy)
    field_in = []
    for c in range(chunks):
        span = pl.ds(c * per, per)
        copy = pltpu.make_async_copy(field_hbm.at[span], field_buf.at[span], field_sem.at[c])
        copy.start()
        field_in.append(copy)

    barrier = pltpu.get_barrier_semaphore()
    for d in range(1, peers):
        pl.semaphore_signal(
            barrier, inc=1, device_id={"lon": lax.rem(me + d, peers)}, device_id_type=pl.DeviceIdType.MESH
        )
    pl.semaphore_signal(barrier, inc=1, device_id={"lat": other}, device_id_type=pl.DeviceIdType.MESH)
    pl.semaphore_wait(barrier, peers)

    def lon_copy(shard, slot, target):
        ref = lon_buf.at[shard, my_half]
        return remote(ref, ref, lon_send.at[slot], lon_recv.at[shard], {"lon": target})

    mate = z * y_size + (1 - y)
    inner = (z == 1) | (z == 2)
    first = 1 + lax.rem(z, 2)
    second = jnp.where(lax.rem(z, 2) == 0, 2 + z // 2, z // 2)
    outward = jnp.where(z == 1, 0, 3)
    lon_in.wait()
    started = [
        lon_copy(me, 0, first * y_size + y),
        lon_copy(me, 1, second * y_size + y),
        lon_copy(me, 2, mate),
    ]
    for copy in started:
        copy.start()

    def lon_arrived(shard):
        ref = lon_buf.at[shard, my_half]
        remote(ref, ref, lon_send.at[0], lon_recv.at[shard], {"lon": mate}).wait_recv()

    def along_z(d):
        return jnp.where(z < 2, lax.rem(z + d, z_size), lax.rem(z + z_size - d, z_size)) * y_size + y

    def pass_copies(d, outwards):
        shard = along_z(d)
        copies = [lon_copy(shard, 2 + d, mate)]
        if outwards:
            copies.append(lon_copy(shard, 5 + d, outward * y_size + y))
        return copies

    def pass_on(d, outwards):
        lon_arrived(along_z(d))
        for copy in pass_copies(d, outwards):
            copy.start()

    for copy in lat_in:
        copy.wait()
    hi, lo = split(lat_buf[...])
    lat_hi[...] = hi
    lat_lo[...] = lo

    def pair_copy(c):
        span = pl.ds(c * per, per)
        return remote(sent.at[span], got.at[span], pair_send.at[c], pair_recv.at[c], {"lat": other})

    def contract(c):
        field_in[c].wait()
        span = pl.ds(c * per, per)
        hi, lo = split(field_buf[span].reshape(per * rows, depth))
        total = dot(hi, lat_hi[...]) + dot(hi, lat_lo[...]) + dot(lo, lat_hi[...])
        sent[span] = total[:, width:].reshape(per, rows, width)
        pair_copy(c).start()
        mine[span] = total[:, :width].reshape(per, rows, width)

    def level_at(z_there, y_there):
        return y_there * z_size + lax.rem(z_there, 2) * 2 + z_there // 2

    my_level = level_at(z, y)

    def one_copy(z_there, y_there):
        return remote(
            mine.at[level_at(z_there, y_there)], level_buf.at[me],
            one_send.at[z_there * y_size + y_there], one_recv.at[me], {"lon": z_there * y_size + y_there},
        )

    def spread(c):
        pair_copy(c).wait_recv()
        span = pl.ds(c * per, per)
        mine[span] = mine[span] + got[span]
        for along in (3, 2, 1):
            one_copy(flipped(along, 0)[0], c).start()

        @pl.when(y != c)
        def _():
            one_copy(z, c).start()

        @pl.when(y == c)
        def _():
            level_buf[me] = mine[my_level]

    for c in range(chunks):
        contract(c)
        if c:
            spread(c - 1)

    @pl.when(inner)
    def _():
        pass_on(1, True)
        pass_on(2, True)
        pass_on(3, False)

    @pl.when(~inner)
    def _():
        pass_on(1, False)

    spread(chunks - 1)

    @pl.when(~inner)
    def _():
        pass_on(2, False)
        pass_on(3, False)

    for d in range(z_size):
        lon_arrived(lax.rem(z + d, z_size) * y_size + (1 - y))
    all_halves = lon_buf.at[:, my_half]
    share = remote(all_halves, all_halves, share_send, share_recv, {"lat": other})
    share.start()
    share.wait_recv()
    step = lon_hi.shape[1] // 4
    for block in range(lon_hi.shape[0] // step):
        cols = pl.ds(block * step, step)
        hi, lo = split(lon_buf[:, :, cols].reshape(peers * rows, step).T)
        lon_hi[cols] = hi
        lon_lo[cols] = lo

    for d in range(1, peers):
        source = lax.rem(me + d, peers)
        remote(mine.at[0], level_buf.at[source], one_send.at[0], one_recv.at[source], {"lon": source}).wait_recv()
    hi, lo = split(level_buf[...].reshape(peers * rows, width))

    def two_copy(z_there, y_there):
        target = z_there * y_size + y_there
        return remote(core_buf.at[target], out_ref.at[my_level], two_send.at[target], two_recv.at[me], {"lon": target})

    block = core_buf.shape[1]
    for along in (3, 2, 1, 0):
        z_there, _ = flipped(along, 0)
        cols = pl.ds(pl.multiple_of(z_there * y_size * block, y_size * block), y_size * block)
        total = dot(lon_hi[cols], hi) + dot(lon_hi[cols], lo) + dot(lon_lo[cols], hi)
        core_buf[pl.ds(z_there * y_size, y_size)] = total.reshape(y_size, block, width)
        for across in (1, 0):
            if along or across:
                two_copy(*flipped(along, across)).start()
    out_ref[my_level] = core_buf[me]

    for copy in started:
        copy.wait_send()
    for d in range(1, z_size):
        pass_copies(d, False)[0].wait_send()

    @pl.when(inner)
    def _():
        for d in (1, 2):
            pass_copies(d, True)[1].wait_send()

    share.wait_send()
    for c in range(chunks):
        pair_copy(c).wait_send()
    away = [(along, across) for along in range(z_size) for across in range(y_size) if along or across]
    for place in away:
        one_copy(*flipped(*place)).wait_send()
    for place in away:
        z_there, y_there = flipped(*place)
        source = z_there * y_size + y_there
        remote(
            core_buf.at[0], out_ref.at[level_at(z_there, y_there)], two_send.at[0], two_recv.at[source], {"lon": source}
        ).wait_recv()
    for place in away:
        two_copy(*flipped(*place)).wait_send()


def exchanged(field, longitude_matrix, latitude_matrix):
    levels, rows, depth = field.shape
    rank = longitude_matrix.shape[1]
    columns = latitude_matrix.shape[1]
    peers = lax.axis_size("lon")
    width = columns // lax.axis_size("lat")
    block = rank // peers
    chunks, y_size = 2, 2
    z_size = peers // y_size
    dma = pltpu.SemaphoreType.DMA
    flops = 6 * (levels * rows * depth * columns + peers * rows * rank * width)
    return pl.pallas_call(
        functools.partial(kernel, chunks, y_size),
        out_shape=jax.ShapeDtypeStruct((levels, block, width), F32),
        in_specs=[pl.BlockSpec(memory_space=pltpu.HBM)] * 3,
        out_specs=pl.BlockSpec(memory_space=pltpu.VMEM),
        scratch_shapes=[
            pltpu.VMEM((levels, rows, depth), F32),
            pltpu.VMEM((depth, columns), F32),
            pltpu.VMEM((peers, rows, rank), F32),
            pltpu.VMEM((depth, columns), BF16),
            pltpu.VMEM((depth, columns), BF16),
            pltpu.VMEM((rank, peers * rows), BF16),
            pltpu.VMEM((rank, peers * rows), BF16),
            pltpu.VMEM((levels, rows, width), F32),
            pltpu.VMEM((levels, rows, width), F32),
            pltpu.VMEM((levels, rows, width), F32),
            pltpu.VMEM((peers, rows, width), F32),
            pltpu.VMEM((peers, block, width), F32),
            dma((chunks,)), dma((2,)), dma(()), dma((chunks,)), dma((chunks,)),
            dma((2 * z_size,)), dma((peers,)), dma(()), dma(()),
            dma((peers,)), dma((peers,)), dma((peers,)), dma((peers,)),
        ],
        compiler_params=pltpu.CompilerParams(
            collective_id=0, has_side_effects=True, vmem_limit_bytes=60 * 1024 * 1024
        ),
        cost_estimate=pl.CostEstimate(
            flops=flops, bytes_accessed=4 * (field.size + longitude_matrix.size + latitude_matrix.size), transcendentals=0
        ),
    )(field, longitude_matrix, latitude_matrix)


def collected(field, longitude_matrix, latitude_matrix):
    highest = lax.Precision.HIGHEST
    reduced = lax.psum_scatter(
        jnp.einsum("mb,vnm->bvn", latitude_matrix, field, precision=highest),
        "lat", scatter_dimension=0, tiled=True,
    )
    parts = lax.psum_scatter(
        jnp.einsum("bvn,na->avb", reduced, longitude_matrix, precision=highest),
        "lon", scatter_dimension=0, tiled=True,
    )
    return jnp.transpose(parts, (1, 0, 2))


def body(field, longitude_matrix, latitude_matrix):
    if lax.axis_size("lat") == 2 and lax.axis_size("lon") == 8 == field.shape[0]:
        return exchanged(field, longitude_matrix, latitude_matrix)
    return collected(field, longitude_matrix, latitude_matrix)


def solution(mesh):
    in_specs = (P("hours", "lon", "lat"), P(("hours", "lon"), None), P(("hours", "lat"), None))
    out_specs = P("hours", "lon", "lat")
    return jax.shard_map(body, mesh=mesh, in_specs=in_specs, out_specs=out_specs, check_vma=False)
```

```python
import functools

import jax
import jax.numpy as jnp
from jax import lax
from jax.experimental import pallas as pl
from jax.experimental.pallas import tpu as pltpu
from jax.sharding import PartitionSpec as P

F32 = jnp.float32
BF16 = jnp.bfloat16


def split(x):
    hi = x.astype(BF16)
    return hi, (x - hi.astype(F32)).astype(BF16)


def dot(a, b):
    return jnp.dot(a, b, preferred_element_type=F32)


def kernel(
    chunks, y_size,
    field_hbm, lon_hbm, lat_hbm, out_ref,
    field_buf, lat_buf, lon_buf, lat_hi, lat_lo, lon_hi, lon_lo,
    mine, sent, got, level_buf, core_buf,
    field_sem, lat_sem, lon_sem, pair_send, pair_recv,
    lon_send, lon_recv, share_send, share_recv,
    one_send, one_recv, two_send, two_recv,
):
    levels, rows, depth = field_buf.shape
    width = mine.shape[2]
    peers = levels
    half = rows // 2
    z_size = peers // y_size
    per = levels // chunks
    me = lax.axis_index("lon")
    core = lax.axis_index("lat")
    other = 1 - core
    z, y = me // y_size, lax.rem(me, y_size)

    def flipped(along, across):
        z_there = (z, z + 1 - 2 * lax.rem(z, 2), lax.rem(z + 2, z_size), z_size - 1 - z)[along]
        return z_there, (y, 1 - y)[across]

    def remote(src, dst, send_sem, recv_sem, target):
        return pltpu.make_async_remote_copy(
            src_ref=src, dst_ref=dst, send_sem=send_sem, recv_sem=recv_sem,
            device_id=target, device_id_type=pl.DeviceIdType.MESH,
        )

    my_half = pl.ds(pl.multiple_of(core * half, half), half)
    lon_in = pltpu.make_async_copy(lon_hbm.at[my_half], lon_buf.at[me, my_half], lon_sem)
    lon_in.start()
    lat_in = []
    for part, who in ((0, core), (1, other)):
        columns = pl.ds(pl.multiple_of(who * width, width), width)
        copy = pltpu.make_async_copy(
            lat_hbm.at[:, columns], lat_buf.at[:, pl.ds(part * width, width)], lat_sem.at[part]
        )
        copy.start()
        lat_in.append(copy)
    field_in = []
    for c in range(chunks):
        span = pl.ds(c * per, per)
        copy = pltpu.make_async_copy(field_hbm.at[span], field_buf.at[span], field_sem.at[c])
        copy.start()
        field_in.append(copy)

    barrier = pltpu.get_barrier_semaphore()
    for d in range(1, peers):
        pl.semaphore_signal(
            barrier, inc=1, device_id={"lon": lax.rem(me + d, peers)}, device_id_type=pl.DeviceIdType.MESH
        )
    pl.semaphore_signal(barrier, inc=1, device_id={"lat": other}, device_id_type=pl.DeviceIdType.MESH)
    pl.semaphore_wait(barrier, peers)

    def lon_copy(shard, slot, target):
        ref = lon_buf.at[shard, my_half]
        return remote(ref, ref, lon_send.at[slot], lon_recv.at[shard], {"lon": target})

    mate = z * y_size + (1 - y)
    inner = (z == 1) | (z == 2)
    first = 1 + lax.rem(z, 2)
    second = jnp.where(lax.rem(z, 2) == 0, 2 + z // 2, z // 2)
    outward = jnp.where(z == 1, 0, 3)
    lon_in.wait()
    started = [
        lon_copy(me, 0, first * y_size + y),
        lon_copy(me, 1, second * y_size + y),
        lon_copy(me, 2, mate),
    ]
    for copy in started:
        copy.start()

    def lon_arrived(shard):
        ref = lon_buf.at[shard, my_half]
        remote(ref, ref, lon_send.at[0], lon_recv.at[shard], {"lon": mate}).wait_recv()

    def along_z(d):
        return jnp.where(z < 2, lax.rem(z + d, z_size), lax.rem(z + z_size - d, z_size)) * y_size + y

    def pass_copies(d, outwards):
        shard = along_z(d)
        copies = [lon_copy(shard, 2 + d, mate)]
        if outwards:
            copies.append(lon_copy(shard, 5 + d, outward * y_size + y))
            copies.append(lon_copy(shard, 7 + d, outward * y_size + (1 - y)))
        return copies

    def pass_on(d, outwards):
        lon_arrived(along_z(d))
        for copy in pass_copies(d, outwards):
            copy.start()

    for copy in lat_in:
        copy.wait()
    hi, lo = split(lat_buf[...])
    lat_hi[...] = hi
    lat_lo[...] = lo

    def pair_copy(c):
        span = pl.ds(c * per, per)
        return remote(sent.at[span], got.at[span], pair_send.at[c], pair_recv.at[c], {"lat": other})

    def contract(c):
        field_in[c].wait()
        span = pl.ds(c * per, per)
        hi, lo = split(field_buf[span].reshape(per * rows, depth))
        total = dot(hi, lat_hi[...]) + dot(hi, lat_lo[...]) + dot(lo, lat_hi[...])
        sent[span] = total[:, width:].reshape(per, rows, width)
        pair_copy(c).start()
        mine[span] = total[:, :width].reshape(per, rows, width)

    def level_at(z_there, y_there):
        return y_there * z_size + lax.rem(z_there, 2) * 2 + z_there // 2

    my_level = level_at(z, y)

    def one_copy(z_there, y_there):
        return remote(
            mine.at[level_at(z_there, y_there)], level_buf.at[me],
            one_send.at[z_there * y_size + y_there], one_recv.at[me], {"lon": z_there * y_size + y_there},
        )

    def spread(c):
        pair_copy(c).wait_recv()
        span = pl.ds(c * per, per)
        mine[span] = mine[span] + got[span]
        for along in (3, 2, 1):
            one_copy(flipped(along, 0)[0], c).start()

        @pl.when(y != c)
        def _():
            one_copy(z, c).start()

        @pl.when(y == c)
        def _():
            level_buf[me] = mine[my_level]

    for c in range(chunks):
        contract(c)

    @pl.when(inner)
    def _():
        pass_on(1, True)
        pass_on(2, True)
        pass_on(3, False)

    @pl.when(~inner)
    def _():
        pass_on(1, False)

    for c in range(chunks - 1):
        spread(c)
    spread(chunks - 1)

    @pl.when(~inner)
    def _():
        lon_arrived(along_z(2))
        lon_arrived(along_z(3))

    for d in range(z_size):
        lon_arrived(lax.rem(z + d, z_size) * y_size + (1 - y))
    all_halves = lon_buf.at[:, my_half]
    share = remote(all_halves, all_halves, share_send, share_recv, {"lat": other})
    share.start()
    share.wait_recv()
    step = lon_hi.shape[1] // 4
    for block in range(lon_hi.shape[0] // step):
        cols = pl.ds(block * step, step)
        hi, lo = split(lon_buf[:, :, cols].reshape(peers * rows, step).T)
        lon_hi[cols] = hi
        lon_lo[cols] = lo

    for d in range(1, peers):
        source = lax.rem(me + d, peers)
        remote(mine.at[0], level_buf.at[source], one_send.at[0], one_recv.at[source], {"lon": source}).wait_recv()
    hi, lo = split(level_buf[...].reshape(peers * rows, width))

    def two_copy(z_there, y_there):
        target = z_there * y_size + y_there
        return remote(core_buf.at[target], out_ref.at[my_level], two_send.at[target], two_recv.at[me], {"lon": target})

    block = core_buf.shape[1]
    for along in (3, 2, 1, 0):
        z_there, _ = flipped(along, 0)
        cols = pl.ds(pl.multiple_of(z_there * y_size * block, y_size * block), y_size * block)
        total = dot(lon_hi[cols], hi) + dot(lon_hi[cols], lo) + dot(lon_lo[cols], hi)
        core_buf[pl.ds(z_there * y_size, y_size)] = total.reshape(y_size, block, width)
        for across in (1, 0):
            if along or across:
                two_copy(*flipped(along, across)).start()
    out_ref[my_level] = core_buf[me]

    for copy in started:
        copy.wait_send()
    pass_copies(1, False)[0].wait_send()

    @pl.when(inner)
    def _():
        for copy in pass_copies(1, True)[1:] + pass_copies(2, True) + pass_copies(3, False):
            copy.wait_send()

    share.wait_send()
    for c in range(chunks):
        pair_copy(c).wait_send()
    away = [(along, across) for along in range(z_size) for across in range(y_size) if along or across]
    for place in away:
        one_copy(*flipped(*place)).wait_send()
    for place in away:
        z_there, y_there = flipped(*place)
        source = z_there * y_size + y_there
        remote(
            core_buf.at[0], out_ref.at[level_at(z_there, y_there)], two_send.at[0], two_recv.at[source], {"lon": source}
        ).wait_recv()
    for place in away:
        two_copy(*flipped(*place)).wait_send()


def exchanged(field, longitude_matrix, latitude_matrix):
    levels, rows, depth = field.shape
    rank = longitude_matrix.shape[1]
    columns = latitude_matrix.shape[1]
    peers = lax.axis_size("lon")
    width = columns // lax.axis_size("lat")
    block = rank // peers
    chunks, y_size = 2, 2
    z_size = peers // y_size
    dma = pltpu.SemaphoreType.DMA
    flops = 6 * (levels * rows * depth * columns + peers * rows * rank * width)
    return pl.pallas_call(
        functools.partial(kernel, chunks, y_size),
        out_shape=jax.ShapeDtypeStruct((levels, block, width), F32),
        in_specs=[pl.BlockSpec(memory_space=pltpu.HBM)] * 3,
        out_specs=pl.BlockSpec(memory_space=pltpu.VMEM),
        scratch_shapes=[
            pltpu.VMEM((levels, rows, depth), F32),
            pltpu.VMEM((depth, columns), F32),
            pltpu.VMEM((peers, rows, rank), F32),
            pltpu.VMEM((depth, columns), BF16),
            pltpu.VMEM((depth, columns), BF16),
            pltpu.VMEM((rank, peers * rows), BF16),
            pltpu.VMEM((rank, peers * rows), BF16),
            pltpu.VMEM((levels, rows, width), F32),
            pltpu.VMEM((levels, rows, width), F32),
            pltpu.VMEM((levels, rows, width), F32),
            pltpu.VMEM((peers, rows, width), F32),
            pltpu.VMEM((peers, block, width), F32),
            dma((chunks,)), dma((2,)), dma(()), dma((chunks,)), dma((chunks,)),
            dma((2 * z_size + 2,)), dma((peers,)), dma(()), dma(()),
            dma((peers,)), dma((peers,)), dma((peers,)), dma((peers,)),
        ],
        compiler_params=pltpu.CompilerParams(
            collective_id=0, has_side_effects=True, vmem_limit_bytes=40 * 1024 * 1024
        ),
        cost_estimate=pl.CostEstimate(
            flops=flops, bytes_accessed=4 * (field.size + longitude_matrix.size + latitude_matrix.size), transcendentals=0
        ),
    )(*[pltpu.with_memory_space_constraint(x, pltpu.HBM) for x in (field, longitude_matrix, latitude_matrix)])


def collected(field, longitude_matrix, latitude_matrix):
    highest = lax.Precision.HIGHEST
    reduced = lax.psum_scatter(
        jnp.einsum("mb,vnm->bvn", latitude_matrix, field, precision=highest),
        "lat", scatter_dimension=0, tiled=True,
    )
    parts = lax.psum_scatter(
        jnp.einsum("bvn,na->avb", reduced, longitude_matrix, precision=highest),
        "lon", scatter_dimension=0, tiled=True,
    )
    return jnp.transpose(parts, (1, 0, 2))


def body(field, longitude_matrix, latitude_matrix):
    if lax.axis_size("lat") == 2 and lax.axis_size("lon") == 8 == field.shape[0]:
        return exchanged(field, longitude_matrix, latitude_matrix)
    return collected(field, longitude_matrix, latitude_matrix)


def solution(mesh):
    in_specs = (P("hours", "lon", "lat"), P(("hours", "lon"), None), P(("hours", "lat"), None))
    out_specs = P("hours", "lon", "lat")
    return jax.shard_map(body, mesh=mesh, in_specs=in_specs, out_specs=out_specs, check_vma=False)
```

```python
import functools

import jax
import jax.numpy as jnp
from jax import lax
from jax.experimental import pallas as pl
from jax.experimental.pallas import tpu as pltpu
from jax.sharding import PartitionSpec as P

F32 = jnp.float32
BF16 = jnp.bfloat16


def split(x):
    hi = x.astype(BF16)
    return hi, (x - hi.astype(F32)).astype(BF16)


def dot(a, b):
    return jnp.dot(a, b, preferred_element_type=F32)


def kernel(
    chunks, y_size,
    field_hbm, lon_hbm, lat_hbm, out_ref,
    field_buf, lat_buf, lon_buf, lat_all, lon_hi, lon_lo,
    mine, sent, got, level_buf, core_buf,
    field_sem, lat_sem, lon_sem, pair_send, pair_recv,
    lon_send, lon_recv, share_send, share_recv,
    one_send, one_recv, two_send, two_recv,
):
    levels, rows, depth = field_buf.shape
    width = mine.shape[2]
    peers = levels
    half = rows // 2
    z_size = peers // y_size
    per = levels // chunks
    me = lax.axis_index("lon")
    core = lax.axis_index("lat")
    other = 1 - core
    z, y = me // y_size, lax.rem(me, y_size)

    def flipped(along, across):
        z_there = (z, z + 1 - 2 * lax.rem(z, 2), lax.rem(z + 2, z_size), z_size - 1 - z)[along]
        return z_there, (y, 1 - y)[across]

    def remote(src, dst, send_sem, recv_sem, target):
        return pltpu.make_async_remote_copy(
            src_ref=src, dst_ref=dst, send_sem=send_sem, recv_sem=recv_sem,
            device_id=target, device_id_type=pl.DeviceIdType.MESH,
        )

    my_half = pl.ds(pl.multiple_of(core * half, half), half)
    lon_in = pltpu.make_async_copy(lon_hbm.at[my_half], lon_buf.at[me, my_half], lon_sem)
    lon_in.start()
    lat_in = []
    for part, who in ((0, core), (1, other)):
        columns = pl.ds(pl.multiple_of(who * width, width), width)
        copy = pltpu.make_async_copy(
            lat_hbm.at[:, columns], lat_buf.at[:, pl.ds(part * width, width)], lat_sem.at[part]
        )
        copy.start()
        lat_in.append(copy)
    field_in = []
    for c in range(chunks):
        span = pl.ds(c * per, per)
        copy = pltpu.make_async_copy(field_hbm.at[span], field_buf.at[span], field_sem.at[c])
        copy.start()
        field_in.append(copy)

    barrier = pltpu.get_barrier_semaphore()
    for d in range(1, peers):
        pl.semaphore_signal(
            barrier, inc=1, device_id={"lon": lax.rem(me + d, peers)}, device_id_type=pl.DeviceIdType.MESH
        )
    pl.semaphore_signal(barrier, inc=1, device_id={"lat": other}, device_id_type=pl.DeviceIdType.MESH)

    def lon_copy(shard, slot, target):
        ref = lon_buf.at[shard, my_half]
        return remote(ref, ref, lon_send.at[slot], lon_recv.at[shard], {"lon": target})

    mate = z * y_size + (1 - y)
    inner = (z == 1) | (z == 2)
    first = 1 + lax.rem(z, 2)
    second = jnp.where(lax.rem(z, 2) == 0, 2 + z // 2, z // 2)
    outward = jnp.where(z == 1, 0, 3)
    for copy in lat_in:
        copy.wait()
    hi, lo = split(lat_buf[...])
    for place, piece in enumerate((hi, lo, hi)):
        lat_all[pl.ds(place * depth, depth)] = piece
    pl.semaphore_wait(barrier, peers)
    lon_in.wait()
    started = [
        lon_copy(me, 0, first * y_size + y),
        lon_copy(me, 1, second * y_size + y),
        lon_copy(me, 2, mate),
    ]
    for copy in started:
        copy.start()

    def lon_arrived(shard):
        ref = lon_buf.at[shard, my_half]
        remote(ref, ref, lon_send.at[0], lon_recv.at[shard], {"lon": mate}).wait_recv()

    def along_z(d):
        return jnp.where(z < 2, lax.rem(z + d, z_size), lax.rem(z + z_size - d, z_size)) * y_size + y

    def pass_copies(d, outwards):
        shard = along_z(d)
        copies = [lon_copy(shard, 2 + d, mate)]
        if outwards:
            copies.append(lon_copy(shard, 5 + d, outward * y_size + y))
            copies.append(lon_copy(shard, 7 + d, outward * y_size + (1 - y)))
        return copies

    def pass_on(d, outwards):
        lon_arrived(along_z(d))
        for copy in pass_copies(d, outwards):
            copy.start()


    def pair_copy(c):
        span = pl.ds(c * per, per)
        return remote(sent.at[span], got.at[span], pair_send.at[c], pair_recv.at[c], {"lat": other})

    def contract(c):
        field_in[c].wait()
        span = pl.ds(c * per, per)
        hi, lo = split(field_buf[span].reshape(per * rows, depth))
        total = dot(jnp.concatenate([hi, hi, lo], axis=1), lat_all[...])
        sent[span] = total[:, width:].reshape(per, rows, width)
        pair_copy(c).start()
        mine[span] = total[:, :width].reshape(per, rows, width)

    def level_at(z_there, y_there):
        return y_there * z_size + lax.rem(z_there, 2) * 2 + z_there // 2

    my_level = level_at(z, y)

    def one_copy(z_there, y_there):
        return remote(
            mine.at[level_at(z_there, y_there)], level_buf.at[me],
            one_send.at[z_there * y_size + y_there], one_recv.at[me], {"lon": z_there * y_size + y_there},
        )

    def spread(c):
        pair_copy(c).wait_recv()
        span = pl.ds(c * per, per)
        mine[span] = mine[span] + got[span]
        for along in (3, 2, 1):
            one_copy(flipped(along, 0)[0], c).start()

        @pl.when(y != c)
        def _():
            one_copy(z, c).start()

        @pl.when(y == c)
        def _():
            level_buf[me] = mine[my_level]

    for c in range(chunks):
        contract(c)

    @pl.when(inner)
    def _():
        pass_on(1, True)
        pass_on(2, True)
        pass_on(3, False)

    @pl.when(~inner)
    def _():
        pass_on(1, False)

    for c in range(chunks - 1):
        spread(c)
    spread(chunks - 1)

    @pl.when(~inner)
    def _():
        lon_arrived(along_z(2))
        lon_arrived(along_z(3))

    for d in range(z_size):
        lon_arrived(lax.rem(z + d, z_size) * y_size + (1 - y))
    all_halves = lon_buf.at[:, my_half]
    share = remote(all_halves, all_halves, share_send, share_recv, {"lat": other})
    share.start()
    share.wait_recv()
    step = lon_hi.shape[1] // 4
    for block in range(lon_hi.shape[0] // step):
        cols = pl.ds(block * step, step)
        hi, lo = split(lon_buf[:, :, cols].reshape(peers * rows, step).T)
        lon_hi[cols] = hi
        lon_lo[cols] = lo

    for d in range(1, peers):
        source = lax.rem(me + d, peers)
        remote(mine.at[0], level_buf.at[source], one_send.at[0], one_recv.at[source], {"lon": source}).wait_recv()
    hi, lo = split(level_buf[...].reshape(peers * rows, width))

    def two_copy(z_there, y_there):
        target = z_there * y_size + y_there
        return remote(core_buf.at[target], out_ref.at[my_level], two_send.at[target], two_recv.at[me], {"lon": target})

    block = core_buf.shape[1]
    for along in (3, 2, 1, 0):
        z_there, _ = flipped(along, 0)
        cols = pl.ds(pl.multiple_of(z_there * y_size * block, y_size * block), y_size * block)
        total = dot(lon_hi[cols], hi) + dot(lon_hi[cols], lo) + dot(lon_lo[cols], hi)
        core_buf[pl.ds(z_there * y_size, y_size)] = total.reshape(y_size, block, width)
        for across in (1, 0):
            if along or across:
                two_copy(*flipped(along, across)).start()
    out_ref[my_level] = core_buf[me]

    for copy in started:
        copy.wait_send()
    pass_copies(1, False)[0].wait_send()

    @pl.when(inner)
    def _():
        for copy in pass_copies(1, True)[1:] + pass_copies(2, True) + pass_copies(3, False):
            copy.wait_send()

    share.wait_send()
    for c in range(chunks):
        pair_copy(c).wait_send()
    away = [(along, across) for along in range(z_size) for across in range(y_size) if along or across]
    for place in away:
        one_copy(*flipped(*place)).wait_send()
    for place in away:
        z_there, y_there = flipped(*place)
        source = z_there * y_size + y_there
        remote(
            core_buf.at[0], out_ref.at[level_at(z_there, y_there)], two_send.at[0], two_recv.at[source], {"lon": source}
        ).wait_recv()
    for place in away:
        two_copy(*flipped(*place)).wait_send()


def exchanged(field, longitude_matrix, latitude_matrix):
    levels, rows, depth = field.shape
    rank = longitude_matrix.shape[1]
    columns = latitude_matrix.shape[1]
    peers = lax.axis_size("lon")
    width = columns // lax.axis_size("lat")
    block = rank // peers
    chunks, y_size = 2, 2
    z_size = peers // y_size
    dma = pltpu.SemaphoreType.DMA
    flops = 6 * (levels * rows * depth * columns + peers * rows * rank * width)
    return pl.pallas_call(
        functools.partial(kernel, chunks, y_size),
        out_shape=jax.ShapeDtypeStruct((levels, block, width), F32),
        in_specs=[pl.BlockSpec(memory_space=pltpu.HBM)] * 3,
        out_specs=pl.BlockSpec(memory_space=pltpu.VMEM),
        scratch_shapes=[
            pltpu.VMEM((levels, rows, depth), F32),
            pltpu.VMEM((depth, columns), F32),
            pltpu.VMEM((peers, rows, rank), F32),
            pltpu.VMEM((3 * depth, columns), BF16),
            pltpu.VMEM((rank, peers * rows), BF16),
            pltpu.VMEM((rank, peers * rows), BF16),
            pltpu.VMEM((levels, rows, width), F32),
            pltpu.VMEM((levels, rows, width), F32),
            pltpu.VMEM((levels, rows, width), F32),
            pltpu.VMEM((peers, rows, width), F32),
            pltpu.VMEM((peers, block, width), F32),
            dma((chunks,)), dma((2,)), dma(()), dma((chunks,)), dma((chunks,)),
            dma((2 * z_size + 2,)), dma((peers,)), dma(()), dma(()),
            dma((peers,)), dma((peers,)), dma((peers,)), dma((peers,)),
        ],
        compiler_params=pltpu.CompilerParams(
            collective_id=0, has_side_effects=True, vmem_limit_bytes=40 * 1024 * 1024
        ),
        cost_estimate=pl.CostEstimate(
            flops=flops, bytes_accessed=4 * (field.size + longitude_matrix.size + latitude_matrix.size), transcendentals=0
        ),
    )(*[pltpu.with_memory_space_constraint(x, pltpu.HBM) for x in (field, longitude_matrix, latitude_matrix)])


def collected(field, longitude_matrix, latitude_matrix):
    highest = lax.Precision.HIGHEST
    reduced = lax.psum_scatter(
        jnp.einsum("mb,vnm->bvn", latitude_matrix, field, precision=highest),
        "lat", scatter_dimension=0, tiled=True,
    )
    parts = lax.psum_scatter(
        jnp.einsum("bvn,na->avb", reduced, longitude_matrix, precision=highest),
        "lon", scatter_dimension=0, tiled=True,
    )
    return jnp.transpose(parts, (1, 0, 2))


def body(field, longitude_matrix, latitude_matrix):
    if lax.axis_size("lat") == 2 and lax.axis_size("lon") == 8 == field.shape[0]:
        return exchanged(field, longitude_matrix, latitude_matrix)
    return collected(field, longitude_matrix, latitude_matrix)


def solution(mesh):
    in_specs = (P("hours", "lon", "lat"), P(("hours", "lon"), None), P(("hours", "lat"), None))
    out_specs = P("hours", "lon", "lat")
    return jax.shard_map(body, mesh=mesh, in_specs=in_specs, out_specs=out_specs, check_vma=False)
```
